32 devices in a mesh: lat: 8 (over y, x, core), lon: 4 (over z).
Axes of the slice: x: 2, y: 2, z: 4, core: 2. Of those that a mesh axis runs over, the one named last changes fastest.
Arguments:
- tracers: float32 [3, 1, 128, 1536], P(None, None, 'lat', 'lon'), may hold values from -6 to 6
- lon_offsets: int32 [128], P('lat'), may hold values from -190 to 190, as said below
- lon_weights: float32 [4, 128], P(None, 'lat'), may hold values from -0.25 to 0.75
- lat_offsets: int32 [128], replicated, may hold values from -4 to 4, as said below
- lat_weights: float32 [4, 128], replicated, may hold values from -0.25 to 0.75
Outputs:
- advected: float32 [3, 1, 128, 1536], P(None, None, 'lat', 'lon')
The draws below stay inside these ranges and needn't reach their ends.
Inputs may be any that keep to these rules, and one draw needn't show every extreme that they name: `lon_offsets`: magnitudes are larger in the polar quarters of the rows; the bound is reached in every draw. `lat_offsets`: the bound is reached in every draw.
All inputs are finite; a program needn't handle non-finite values.
Results may differ from the reference program's by a relative error of at most 0.0003.
Values sent between devices are 32-bit elements; how exact they have to be, the bound alone decides.
A program may use at most 64 MiB of HBM per device.

```python
import jax
import jax.numpy as jnp
from jax import lax

TRACERS = 3
LEVELS = 1
NLAT = 128
NLON = 1536
HALO = 192
LATH = 6


def draw_lon_offsets(key, part):
    rows = jnp.arange(NLAT, dtype=jnp.int32)
    distance = jnp.minimum(rows, NLAT - 1 - rows)
    quarter = NLAT // 4
    reach = 2 + (HALO - 4) * jnp.maximum(0, quarter - distance) // quarter
    drawn = jax.random.randint(key, (NLAT,), 0, 1 << 20, dtype=jnp.int32)
    offsets = drawn % (2 * reach + 1) - reach
    offsets = offsets.at[0].set(HALO - 2).at[NLAT - 1].set(2 - HALO)
    return offsets.astype(jnp.int32)


def draw_lat_offsets(key, part):
    reach = LATH - 2
    drawn = jax.random.randint(jax.random.fold_in(key, 7), (NLAT,), 0, 1 << 20, dtype=jnp.int32)
    offsets = drawn % (2 * reach + 1) - reach
    middle = NLAT // 2
    offsets = offsets.at[middle].set(reach).at[middle + 1].set(-reach)
    return offsets.astype(jnp.int32)


def levels(rng, extent, cuts, smallest, high):
    gain = 1.0
    for dim, parts in cuts:
        steps = jax.random.uniform(jax.random.fold_in(jax.random.fold_in(rng, 6), dim), (parts,), jnp.float32, smallest / len(cuts), high / len(cuts))
        gain = gain * jnp.repeat(jnp.exp(steps), extent[dim] // parts).reshape((-1,) + (1,) * (len(extent) - 1 - dim))
    return gain


def gaussian(key, extent, scale, most, cuts=(), kind=jnp.bfloat16):
    entries = scale * jax.random.normal(key, extent, jnp.float32)
    if cuts:
        entries = entries * levels(key, extent, cuts, -0.22, 0.18)
    return jnp.clip(entries, -most, most).astype(kind)


def setup_inputs(seed: int = 0) -> dict:
    keys = jax.random.split(jax.random.key(seed), 6)
    tracers = gaussian(keys[0], (TRACERS, LEVELS, NLAT, NLON), 1.0, 6.0, ((2, 8), (3, 4)), jnp.float32)
    lon_offsets = draw_lon_offsets(jax.random.fold_in(keys[5], 71), 0)
    lon_weights = jnp.clip(-0.25 + 1.0 * jax.random.uniform(keys[2], (4, NLAT), jnp.float32) ** levels(keys[2], (4, NLAT), ((1, 8),), -0.2, 0.2), -0.25, 0.75)
    lat_offsets = draw_lat_offsets(jax.random.fold_in(keys[5], 71), 0)
    lat_weights = jnp.clip(jax.random.uniform(keys[4], (4, NLAT), jnp.float32, -0.25, 0.75), -0.25, 0.75)
    return {"tracers": tracers, "lon_offsets": lon_offsets, "lon_weights": lon_weights, "lat_offsets": lat_offsets, "lat_weights": lat_weights}


def row_taps(row, shift, taps, base, length):
    total = jnp.zeros(row.shape[:-1] + (length,), jnp.float32)
    for k in range(4):
        start = (base - shift - 1 + k).astype(jnp.int32)
        total = total + taps[k] * lax.dynamic_slice_in_dim(row, start, length, axis=row.ndim - 1)
    return total


def reference(tracers, lon_offsets, lon_weights, lat_offsets, lat_weights):
    nlat = tracers.shape[2]
    nlon = tracers.shape[3]
    fields = tracers.reshape((-1, nlat, nlon))

    def one_field(field):
        padded = jnp.concatenate([field[:, nlon - HALO:], field, field[:, :HALO]], axis=1)
        swept = jax.vmap(lambda r, s, w: row_taps(r, s, w, HALO, nlon), in_axes=(0, 0, 1))(padded, lon_offsets, lon_weights)
        rows = jnp.arange(nlat, dtype=jnp.int32)
        total = jnp.zeros((nlat, nlon), jnp.float32)
        for k in range(4):
            source = jnp.clip(rows - lat_offsets - 1 + k, 0, nlat - 1).astype(jnp.int32)
            total = total + lat_weights[k][:, None] * jnp.take(swept, source, axis=0)
        return total

    result = lax.map(one_field, fields)
    return result.reshape(tracers.shape)
```

```python
import functools

import jax
import jax.numpy as jnp
from jax import lax
from jax.experimental import pallas as pl
from jax.experimental.pallas import tpu as pltpu
from jax.sharding import PartitionSpec as P

MESH = pl.DeviceIdType.MESH
LANES = 128
HALF = 64
SUB = 8
BELOW = 5
ABOVE = 6


def kernel(n_lat, n_lon, nlat, tr, lono, lonw, lato, latw, out,
           own, send_r, send_l, from_l, from_r, ext,
           own_sem, s_lon, r_lon, s_lat, r_lat):
    fields, rows, width = own.shape
    tiles = width // LANES
    ilat = lax.axis_index("lat")
    ilon = lax.axis_index("lon")
    right = lax.rem(ilon + 1, n_lon)
    left = lax.rem(ilon + n_lon - 1, n_lon)
    has_lo = ilat > 0
    has_hi = ilat < n_lat - 1

    barrier = pltpu.get_barrier_semaphore()
    pl.semaphore_signal(barrier, inc=1, device_id=(ilat, right), device_id_type=MESH)
    pl.semaphore_signal(barrier, inc=1, device_id=(ilat, left), device_id_type=MESH)

    @pl.when(has_lo)
    def _():
        pl.semaphore_signal(barrier, inc=1, device_id=(ilat - 1, ilon), device_id_type=MESH)

    @pl.when(has_hi)
    def _():
        pl.semaphore_signal(barrier, inc=1, device_id=(ilat + 1, ilon), device_id_type=MESH)

    load = pltpu.make_async_copy(tr, own, own_sem)
    load.start()

    @pl.when(jnp.logical_not(has_lo))
    def _():
        ext[:, 0:SUB, :] = jnp.zeros((fields, SUB, width), jnp.float32)

    @pl.when(jnp.logical_not(has_hi))
    def _():
        ext[:, SUB + rows:, :] = jnp.zeros((fields, SUB, width), jnp.float32)

    lane8 = lax.broadcasted_iota(jnp.int32, (SUB, LANES), 1)
    upper8 = lane8 >= HALF
    load.wait()
    for f in range(fields):
        last = width - LANES
        send_r[f, 0:rows, :] = own[f, :, last:]
        a = own[f, 0:SUB, last - LANES:last]
        b = own[f, SUB:rows, last - LANES:last]
        send_r[f, rows:, :] = jnp.where(upper8, a, pltpu.roll(b, HALF, 1))
        send_l[f, 0:rows, :] = own[f, :, 0:LANES]
        a = own[f, 0:SUB, LANES:2 * LANES]
        b = own[f, SUB:rows, LANES:2 * LANES]
        send_l[f, rows:, :] = jnp.where(upper8, pltpu.roll(b, HALF, 1), a)

    pl.semaphore_wait(barrier, 2 + has_lo.astype(jnp.int32) + has_hi.astype(jnp.int32))

    lon_copies = []
    for f in range(fields):
        to_r = pltpu.make_async_remote_copy(
            src_ref=send_r.at[f], dst_ref=from_l.at[f], send_sem=s_lon.at[0, f],
            recv_sem=r_lon.at[0, f], device_id=(ilat, right), device_id_type=MESH)
        to_l = pltpu.make_async_remote_copy(
            src_ref=send_l.at[f], dst_ref=from_r.at[f], send_sem=s_lon.at[1, f],
            recv_sem=r_lon.at[1, f], device_id=(ilat, left), device_id_type=MESH)
        to_r.start()
        to_l.start()
        lon_copies.append((to_r, to_l))

    row = lax.broadcasted_iota(jnp.int32, (rows, 1), 0)
    start = ilat * rows

    def column(values, first):
        lanes = values.shape[1]
        pick = (lax.broadcasted_iota(jnp.int32, (rows, lanes), 1)
                == first + lax.broadcasted_iota(jnp.int32, (rows, lanes), 0))
        return jnp.sum(jnp.where(pick, values, 0.0), axis=1, keepdims=True)

    lon_off = column(lono[...].astype(jnp.float32), 0).astype(jnp.int32)
    lon_w = [column(lonw[k:k + 1, :], 0) for k in range(4)]
    lat_off = column(lato[...].astype(jnp.float32), start).astype(jnp.int32)
    lat_w = [column(latw[k:k + 1, :], start) for k in range(4)]

    source = [jnp.clip(start + row - lat_off - 1 + k, 0, nlat - 1) - start for k in range(4)]

    def coefficient(s):
        total = jnp.zeros((rows, 1), jnp.float32)
        for k in range(4):
            total = total + jnp.where(source[k] == s, lat_w[k], 0.0)
        return total

    coef = {s: coefficient(s) for s in range(-BELOW, rows + ABOVE)}

    first = jnp.broadcast_to(2 * LANES - 1 - lon_off, (rows, LANES))
    coarse = first >> 7
    fine = first & (LANES - 1)
    lane = lax.broadcasted_iota(jnp.int32, (rows, LANES), 1)
    index = (lane + fine) & (LANES - 1)
    inside = lane < LANES - fine
    is_q = [coarse == q for q in range(3)]

    def lat_copies(f):
        up = pltpu.make_async_remote_copy(
            src_ref=ext.at[f, pl.ds(rows, SUB)], dst_ref=ext.at[f, pl.ds(0, SUB)],
            send_sem=s_lat.at[0, f], recv_sem=r_lat.at[0, f],
            device_id=(ilat + 1, ilon), device_id_type=MESH)
        down = pltpu.make_async_remote_copy(
            src_ref=ext.at[f, pl.ds(SUB, SUB)], dst_ref=ext.at[f, pl.ds(SUB + rows, SUB)],
            send_sem=s_lat.at[1, f], recv_sem=r_lat.at[1, f],
            device_id=(ilat - 1, ilon), device_id_type=MESH)
        return up, down

    partial = []
    for f in range(fields):
        to_r, to_l = lon_copies[f]
        to_r.wait_recv()
        to_l.wait_recv()
        tail_l = from_l[f, rows:, :]
        tail_r = from_r[f, rows:, :]
        x = [jnp.concatenate([tail_l, pltpu.roll(tail_l, HALF, 1)], axis=0), from_l[f, 0:rows, :]]
        x += [own[f, :, i * LANES:(i + 1) * LANES] for i in range(tiles)]
        x += [from_r[f, 0:rows, :], jnp.concatenate([tail_r, pltpu.roll(tail_r, HALF, 1)], axis=0)]
        z = []
        for t in range(tiles + 2):
            y = x[min(t + 3, tiles + 3)]
            for q in (2, 1, 0):
                y = jnp.where(is_q[q], x[t + q], y)
            z.append(jnp.take_along_axis(y, index, axis=1, mode="promise_in_bounds"))
        b = [jnp.where(inside, z[t], z[t + 1]) for t in range(tiles + 1)]
        sums = [lon_w[0] * b[t] for t in range(tiles)]
        for k in range(1, 4):
            moved = [pltpu.roll(v, LANES - k, 1) for v in b]
            for t in range(tiles):
                sums[t] = sums[t] + lon_w[k] * jnp.where(lane < LANES - k, moved[t], moved[t + 1])
        for t in range(tiles):
            ext[f, SUB:SUB + rows, t * LANES:(t + 1) * LANES] = sums[t]
        up, down = lat_copies(f)
        pl.when(has_hi)(up.start)
        pl.when(has_lo)(down.start)

    for f in range(fields):
        low = jnp.zeros((SUB, width), jnp.float32)
        high = jnp.zeros((SUB, width), jnp.float32)
        for s in range(rows):
            line = ext[f, SUB + s:SUB + s + 1, :]
            if s < SUB + ABOVE:
                low = low + coef[s][:SUB] * line
            if s >= SUB - BELOW:
                high = high + coef[s][SUB:] * line
        partial.append((low, high))

    for f in range(fields):
        low, high = partial[f]
        up, down = lat_copies(f)
        pl.when(has_lo)(up.wait_recv)
        pl.when(has_hi)(down.wait_recv)
        for s in range(-BELOW, 0):
            low = low + coef[s][:SUB] * ext[f, SUB + s:SUB + s + 1, :]
        for s in range(rows, rows + ABOVE):
            high = high + coef[s][SUB:] * ext[f, SUB + s:SUB + s + 1, :]
        out[f, 0:SUB, :] = low
        out[f, SUB:rows, :] = high

    for f in range(fields):
        for copy in lon_copies[f]:
            copy.wait_send()
        up, down = lat_copies(f)
        pl.when(has_hi)(up.wait_send)
        pl.when(has_lo)(down.wait_send)


def per_device(n_lat, n_lon, tracers, lon_offsets, lon_weights, lat_offsets, lat_weights):
    rows, width = tracers.shape[2:]
    fields = tracers.shape[0] * tracers.shape[1]
    nlat = lat_offsets.shape[0]
    vmem = pl.BlockSpec(memory_space=pltpu.VMEM)
    out = pl.pallas_call(
        functools.partial(kernel, n_lat, n_lon, nlat),
        out_shape=jax.ShapeDtypeStruct((fields, rows, width), jnp.float32),
        in_specs=[pl.BlockSpec(memory_space=pl.ANY)] + [vmem] * 4,
        out_specs=vmem,
        scratch_shapes=[
            pltpu.VMEM((fields, rows, width), jnp.float32),
            pltpu.VMEM((fields, rows + SUB, LANES), jnp.float32),
            pltpu.VMEM((fields, rows + SUB, LANES), jnp.float32),
            pltpu.VMEM((fields, rows + SUB, LANES), jnp.float32),
            pltpu.VMEM((fields, rows + SUB, LANES), jnp.float32),
            pltpu.VMEM((fields, rows + 2 * SUB, width), jnp.float32),
            pltpu.SemaphoreType.DMA,
            pltpu.SemaphoreType.DMA((2, fields)),
            pltpu.SemaphoreType.DMA((2, fields)),
            pltpu.SemaphoreType.DMA((2, fields)),
            pltpu.SemaphoreType.DMA((2, fields)),
        ],
        compiler_params=pltpu.CompilerParams(collective_id=0, has_side_effects=True),
    )(
        tracers.reshape(fields, rows, width),
        lon_offsets.reshape(1, rows),
        lon_weights,
        lat_offsets.reshape(1, nlat),
        lat_weights,
    )
    return out.reshape(tracers.shape)


def solution(mesh):
    return jax.shard_map(
        functools.partial(per_device, mesh.shape["lat"], mesh.shape["lon"]),
        mesh=mesh,
        in_specs=(P(None, None, "lat", "lon"), P("lat"), P(None, "lat"), P(), P()),
        out_specs=P(None, None, "lat", "lon"),
        check_vma=False,
    )
```

```python
import functools

import jax
import jax.numpy as jnp
from jax import lax
from jax.experimental import pallas as pl
from jax.experimental.pallas import tpu as pltpu
from jax.sharding import PartitionSpec as P

MESH = pl.DeviceIdType.MESH
LANES = 128
HALF = 64
SUB = 8
BELOW = 5
ABOVE = 6


def kernel(n_lat, n_lon, nlat, tr, lono_in, lonw_in, lato_in, latw_in, out,
           own, lono, lonw, lato, latw, send_r, send_l, from_l, from_r, ext,
           own_sem, s_par, s_lon, r_lon, s_lat, r_lat):
    fields, rows, width = own.shape
    tiles = width // LANES
    ilat = lax.axis_index("lat")
    ilon = lax.axis_index("lon")
    right = lax.rem(ilon + 1, n_lon)
    left = lax.rem(ilon + n_lon - 1, n_lon)
    has_lo = ilat > 0
    has_hi = ilat < n_lat - 1

    barrier = pltpu.get_barrier_semaphore()
    pl.semaphore_signal(barrier, inc=1, device_id=(ilat, right), device_id_type=MESH)
    pl.semaphore_signal(barrier, inc=1, device_id=(ilat, left), device_id_type=MESH)

    @pl.when(has_lo)
    def _():
        pl.semaphore_signal(barrier, inc=1, device_id=(ilat - 1, ilon), device_id_type=MESH)

    @pl.when(has_hi)
    def _():
        pl.semaphore_signal(barrier, inc=1, device_id=(ilat + 1, ilon), device_id_type=MESH)

    load = pltpu.make_async_copy(tr, own, own_sem)
    load.start()
    loads = [
        pltpu.make_async_copy(source, target, s_par.at[i])
        for i, (source, target) in enumerate(
            ((lono_in, lono), (lonw_in, lonw), (lato_in, lato), (latw_in, latw)))
    ]
    for copy in loads:
        copy.start()

    @pl.when(jnp.logical_not(has_lo))
    def _():
        ext[:, 0:SUB, :] = jnp.zeros((fields, SUB, width), jnp.float32)

    @pl.when(jnp.logical_not(has_hi))
    def _():
        ext[:, SUB + rows:, :] = jnp.zeros((fields, SUB, width), jnp.float32)

    lane8 = lax.broadcasted_iota(jnp.int32, (SUB, LANES), 1)
    upper8 = lane8 >= HALF
    load.wait()
    for f in range(fields):
        last = width - LANES
        send_r[f, 0:rows, :] = own[f, :, last:]
        a = own[f, 0:SUB, last - LANES:last]
        b = own[f, SUB:rows, last - LANES:last]
        send_r[f, rows:, :] = jnp.where(upper8, a, pltpu.roll(b, HALF, 1))
        send_l[f, 0:rows, :] = own[f, :, 0:LANES]
        a = own[f, 0:SUB, LANES:2 * LANES]
        b = own[f, SUB:rows, LANES:2 * LANES]
        send_l[f, rows:, :] = jnp.where(upper8, pltpu.roll(b, HALF, 1), a)

    pl.semaphore_wait(barrier, 2 + has_lo.astype(jnp.int32) + has_hi.astype(jnp.int32))

    lon_copies = []
    for f in range(fields):
        to_r = pltpu.make_async_remote_copy(
            src_ref=send_r.at[f], dst_ref=from_l.at[f], send_sem=s_lon.at[0, f],
            recv_sem=r_lon.at[0, f], device_id=(ilat, right), device_id_type=MESH)
        to_l = pltpu.make_async_remote_copy(
            src_ref=send_l.at[f], dst_ref=from_r.at[f], send_sem=s_lon.at[1, f],
            recv_sem=r_lon.at[1, f], device_id=(ilat, left), device_id_type=MESH)
        to_r.start()
        to_l.start()
        lon_copies.append((to_r, to_l))

    for copy in loads:
        copy.wait()

    row = lax.broadcasted_iota(jnp.int32, (rows, 1), 0)
    start = ilat * rows

    def column(values, first):
        lanes = values.shape[1]
        pick = (lax.broadcasted_iota(jnp.int32, (rows, lanes), 1)
                == first + lax.broadcasted_iota(jnp.int32, (rows, lanes), 0))
        return jnp.sum(jnp.where(pick, values, 0.0), axis=1, keepdims=True)

    lon_off = column(lono[...].astype(jnp.float32), 0).astype(jnp.int32)
    lon_w = [column(lonw[k:k + 1, :], 0) for k in range(4)]
    lat_off = column(lato[...].astype(jnp.float32), start).astype(jnp.int32)
    lat_w = [column(latw[k:k + 1, :], start) for k in range(4)]

    source = [jnp.clip(start + row - lat_off - 1 + k, 0, nlat - 1) - start for k in range(4)]

    def coefficient(s):
        total = jnp.zeros((rows, 1), jnp.float32)
        for k in range(4):
            total = total + jnp.where(source[k] == s, lat_w[k], 0.0)
        return total

    coef = {s: coefficient(s) for s in range(-BELOW, rows + ABOVE)}

    first = jnp.broadcast_to(2 * LANES - 1 - lon_off, (rows, LANES))
    coarse = first >> 7
    fine = first & (LANES - 1)
    lane = lax.broadcasted_iota(jnp.int32, (rows, LANES), 1)
    index = (lane + fine) & (LANES - 1)
    inside = lane < LANES - fine
    is_q = [coarse == q for q in range(3)]

    def lat_copies(f):
        up = pltpu.make_async_remote_copy(
            src_ref=ext.at[f, pl.ds(rows, SUB)], dst_ref=ext.at[f, pl.ds(0, SUB)],
            send_sem=s_lat.at[0, f], recv_sem=r_lat.at[0, f],
            device_id=(ilat + 1, ilon), device_id_type=MESH)
        down = pltpu.make_async_remote_copy(
            src_ref=ext.at[f, pl.ds(SUB, SUB)], dst_ref=ext.at[f, pl.ds(SUB + rows, SUB)],
            send_sem=s_lat.at[1, f], recv_sem=r_lat.at[1, f],
            device_id=(ilat - 1, ilon), device_id_type=MESH)
        return up, down

    partial = []
    for f in range(fields):
        to_r, to_l = lon_copies[f]
        to_r.wait_recv()
        to_l.wait_recv()
        tail_l = from_l[f, rows:, :]
        tail_r = from_r[f, rows:, :]
        x = [jnp.concatenate([tail_l, pltpu.roll(tail_l, HALF, 1)], axis=0), from_l[f, 0:rows, :]]
        x += [own[f, :, i * LANES:(i + 1) * LANES] for i in range(tiles)]
        x += [from_r[f, 0:rows, :], jnp.concatenate([tail_r, pltpu.roll(tail_r, HALF, 1)], axis=0)]
        z = []
        for t in range(tiles + 2):
            y = x[min(t + 3, tiles + 3)]
            for q in (2, 1, 0):
                y = jnp.where(is_q[q], x[t + q], y)
            z.append(jnp.take_along_axis(y, index, axis=1, mode="promise_in_bounds"))
        b = [jnp.where(inside, z[t], z[t + 1]) for t in range(tiles + 1)]
        sums = [lon_w[0] * b[t] for t in range(tiles)]
        for k in range(1, 4):
            moved = [pltpu.roll(v, LANES - k, 1) for v in b]
            for t in range(tiles):
                sums[t] = sums[t] + lon_w[k] * jnp.where(lane < LANES - k, moved[t], moved[t + 1])
        for t in range(tiles):
            ext[f, SUB:SUB + rows, t * LANES:(t + 1) * LANES] = sums[t]
        up, down = lat_copies(f)
        pl.when(has_hi)(up.start)
        pl.when(has_lo)(down.start)

    for f in range(fields):
        low = jnp.zeros((SUB, width), jnp.float32)
        high = jnp.zeros((SUB, width), jnp.float32)
        for s in range(rows):
            line = ext[f, SUB + s:SUB + s + 1, :]
            if s < SUB + ABOVE:
                low = low + coef[s][:SUB] * line
            if s >= SUB - BELOW:
                high = high + coef[s][SUB:] * line
        partial.append((low, high))

    for f in range(fields):
        low, high = partial[f]
        up, down = lat_copies(f)
        pl.when(has_lo)(up.wait_recv)
        pl.when(has_hi)(down.wait_recv)
        for s in range(-BELOW, 0):
            low = low + coef[s][:SUB] * ext[f, SUB + s:SUB + s + 1, :]
        for s in range(rows, rows + ABOVE):
            high = high + coef[s][SUB:] * ext[f, SUB + s:SUB + s + 1, :]
        out[f, 0:SUB, :] = low
        out[f, SUB:rows, :] = high

    for f in range(fields):
        for copy in lon_copies[f]:
            copy.wait_send()
        up, down = lat_copies(f)
        pl.when(has_hi)(up.wait_send)
        pl.when(has_lo)(down.wait_send)


def per_device(n_lat, n_lon, tracers, lon_offsets, lon_weights, lat_offsets, lat_weights):
    rows, width = tracers.shape[2:]
    fields = tracers.shape[0] * tracers.shape[1]
    nlat = lat_offsets.shape[0]
    vmem = pl.BlockSpec(memory_space=pltpu.VMEM)
    out = pl.pallas_call(
        functools.partial(kernel, n_lat, n_lon, nlat),
        out_shape=pltpu.VMEM((fields, rows, width), jnp.float32),
        in_specs=[pl.BlockSpec(memory_space=pl.ANY)] * 5,
        out_specs=vmem,
        scratch_shapes=[
            pltpu.VMEM((fields, rows, width), jnp.float32),
            pltpu.VMEM((1, rows), jnp.int32),
            pltpu.VMEM((4, rows), jnp.float32),
            pltpu.VMEM((1, nlat), jnp.int32),
            pltpu.VMEM((4, nlat), jnp.float32),
            pltpu.VMEM((fields, rows + SUB, LANES), jnp.float32),
            pltpu.VMEM((fields, rows + SUB, LANES), jnp.float32),
            pltpu.VMEM((fields, rows + SUB, LANES), jnp.float32),
            pltpu.VMEM((fields, rows + SUB, LANES), jnp.float32),
            pltpu.VMEM((fields, rows + 2 * SUB, width), jnp.float32),
            pltpu.SemaphoreType.DMA,
            pltpu.SemaphoreType.DMA((4,)),
            pltpu.SemaphoreType.DMA((2, fields)),
            pltpu.SemaphoreType.DMA((2, fields)),
            pltpu.SemaphoreType.DMA((2, fields)),
            pltpu.SemaphoreType.DMA((2, fields)),
        ],
        compiler_params=pltpu.CompilerParams(collective_id=0, has_side_effects=True),
    )(
        tracers.reshape(fields, rows, width),
        lon_offsets.reshape(1, rows),
        lon_weights,
        lat_offsets.reshape(1, nlat),
        lat_weights,
    )
    return out.reshape(tracers.shape)


def solution(mesh):
    return jax.shard_map(
        functools.partial(per_device, mesh.shape["lat"], mesh.shape["lon"]),
        mesh=mesh,
        in_specs=(P(None, None, "lat", "lon"), P("lat"), P(None, "lat"), P(), P()),
        out_specs=P(None, None, "lat", "lon"),
        check_vma=False,
    )
```

```python
import functools

import jax
import jax.numpy as jnp
from jax import lax
from jax.experimental import pallas as pl
from jax.experimental.pallas import tpu as pltpu
from jax.sharding import PartitionSpec as P

MESH = pl.DeviceIdType.MESH
LANES = 128
HALF = 64
SUB = 8
BELOW = 5
ABOVE = 6


def kernel(n_lat, n_lon, nlat, tr, lono_in, lonw_in, lato_in, latw_in, out,
           own, lono, lonw, lato, latw, send_r, send_l, from_l, from_r, ext,
           own_sem, s_par, s_lon, r_lon, s_lat, r_lat, ready):
    fields, rows, width = own.shape
    tiles = width // LANES
    ilat = lax.axis_index("lat")
    ilon = lax.axis_index("lon")
    right = lax.rem(ilon + 1, n_lon)
    left = lax.rem(ilon + n_lon - 1, n_lon)
    has_lo = ilat > 0
    has_hi = ilat < n_lat - 1

    barrier = pltpu.get_barrier_semaphore()
    at_first = ilon == 0
    at_last = ilon == n_lon - 1

    def signal(semaphore, lat, lon):
        pl.semaphore_signal(semaphore, inc=1, device_id=(lat, lon), device_id_type=MESH)

    pl.when(at_first)(lambda: signal(barrier, ilat, left))
    pl.when(jnp.logical_not(at_last))(lambda: signal(barrier, ilat, right))
    pl.when(has_hi)(lambda: signal(barrier, ilat + 1, ilon))

    load = pltpu.make_async_copy(tr, own, own_sem)
    load.start()
    loads = [
        pltpu.make_async_copy(source, target, s_par.at[i])
        for i, (source, target) in enumerate(
            ((lono_in, lono), (lonw_in, lonw), (lato_in, lato), (latw_in, latw)))
    ]
    for copy in loads:
        copy.start()

    greeted = has_lo.astype(jnp.int32) + jnp.logical_not(at_first).astype(jnp.int32) + at_last.astype(jnp.int32)
    pl.when(greeted > 0)(lambda: pl.semaphore_wait(barrier, greeted))
    pl.when(at_last)(lambda: signal(ready.at[0], ilat, right))
    pl.when(jnp.logical_not(at_first))(lambda: signal(ready.at[1], ilat, left))
    pl.when(has_lo)(lambda: signal(ready.at[2], ilat - 1, ilon))

    @pl.when(jnp.logical_not(has_lo))
    def _():
        ext[:, 0:SUB, :] = jnp.zeros((fields, SUB, width), jnp.float32)

    @pl.when(jnp.logical_not(has_hi))
    def _():
        ext[:, SUB + rows:, :] = jnp.zeros((fields, SUB, width), jnp.float32)

    lane8 = lax.broadcasted_iota(jnp.int32, (SUB, LANES), 1)
    upper8 = lane8 >= HALF
    load.wait()
    for f in range(fields):
        last = width - LANES
        send_r[f, 0:rows, :] = own[f, :, last:]
        a = own[f, 0:SUB, last - LANES:last]
        b = own[f, SUB:rows, last - LANES:last]
        send_r[f, rows:, :] = jnp.where(upper8, a, pltpu.roll(b, HALF, 1))
        send_l[f, 0:rows, :] = own[f, :, 0:LANES]
        a = own[f, 0:SUB, LANES:2 * LANES]
        b = own[f, SUB:rows, LANES:2 * LANES]
        send_l[f, rows:, :] = jnp.where(upper8, pltpu.roll(b, HALF, 1), a)

    lon_copies = []
    for f in range(fields):
        to_r = pltpu.make_async_remote_copy(
            src_ref=send_r.at[f], dst_ref=from_l.at[f], send_sem=s_lon.at[0, f],
            recv_sem=r_lon.at[0, f], device_id=(ilat, right), device_id_type=MESH)
        to_l = pltpu.make_async_remote_copy(
            src_ref=send_l.at[f], dst_ref=from_r.at[f], send_sem=s_lon.at[1, f],
            recv_sem=r_lon.at[1, f], device_id=(ilat, left), device_id_type=MESH)
        lon_copies.append((to_r, to_l))

    def start_right():
        for to_r, _ in lon_copies:
            to_r.start()

    def start_left():
        for _, to_l in lon_copies:
            to_l.start()

    @pl.when(at_last)
    def _():
        start_right()

    @pl.when(jnp.logical_not(at_first))
    def _():
        start_left()

    @pl.when(jnp.logical_not(at_last))
    def _():
        pl.semaphore_wait(ready.at[1], 1)
        start_right()

    @pl.when(at_first)
    def _():
        pl.semaphore_wait(ready.at[0], 1)
        start_left()

    for copy in loads:
        copy.wait()

    row = lax.broadcasted_iota(jnp.int32, (rows, 1), 0)
    start = ilat * rows

    def column(values, first):
        lanes = values.shape[1]
        pick = (lax.broadcasted_iota(jnp.int32, (rows, lanes), 1)
                == first + lax.broadcasted_iota(jnp.int32, (rows, lanes), 0))
        return jnp.sum(jnp.where(pick, values, 0.0), axis=1, keepdims=True)

    lon_off = column(lono[...].astype(jnp.float32), 0).astype(jnp.int32)
    lon_w = [column(lonw[k:k + 1, :], 0) for k in range(4)]
    lat_off = column(lato[...].astype(jnp.float32), start).astype(jnp.int32)
    lat_w = [column(latw[k:k + 1, :], start) for k in range(4)]

    source = [jnp.clip(start + row - lat_off - 1 + k, 0, nlat - 1) - start for k in range(4)]

    def coefficient(s):
        total = jnp.zeros((rows, 1), jnp.float32)
        for k in range(4):
            total = total + jnp.where(source[k] == s, lat_w[k], 0.0)
        return total

    coef = {s: coefficient(s) for s in range(-BELOW, rows + ABOVE)}

    first = jnp.broadcast_to(2 * LANES - 1 - lon_off, (rows, LANES))
    coarse = first >> 7
    fine = first & (LANES - 1)
    lane = lax.broadcasted_iota(jnp.int32, (rows, LANES), 1)
    index = (lane + fine) & (LANES - 1)
    inside = lane < LANES - fine
    is_q = [coarse == q for q in range(3)]

    def lat_copies(f):
        up = pltpu.make_async_remote_copy(
            src_ref=ext.at[f, pl.ds(rows, SUB)], dst_ref=ext.at[f, pl.ds(0, SUB)],
            send_sem=s_lat.at[0, f], recv_sem=r_lat.at[0, f],
            device_id=(ilat + 1, ilon), device_id_type=MESH)
        down = pltpu.make_async_remote_copy(
            src_ref=ext.at[f, pl.ds(SUB, SUB)], dst_ref=ext.at[f, pl.ds(SUB + rows, SUB)],
            send_sem=s_lat.at[1, f], recv_sem=r_lat.at[1, f],
            device_id=(ilat - 1, ilon), device_id_type=MESH)
        return up, down

    partial = []
    for f in range(fields):
        to_r, to_l = lon_copies[f]
        to_r.wait_recv()
        to_l.wait_recv()
        tail_l = from_l[f, rows:, :]
        tail_r = from_r[f, rows:, :]
        x = [jnp.concatenate([tail_l, pltpu.roll(tail_l, HALF, 1)], axis=0), from_l[f, 0:rows, :]]
        x += [own[f, :, i * LANES:(i + 1) * LANES] for i in range(tiles)]
        x += [from_r[f, 0:rows, :], jnp.concatenate([tail_r, pltpu.roll(tail_r, HALF, 1)], axis=0)]
        z = []
        for t in range(tiles + 2):
            y = x[min(t + 3, tiles + 3)]
            for q in (2, 1, 0):
                y = jnp.where(is_q[q], x[t + q], y)
            z.append(jnp.take_along_axis(y, index, axis=1, mode="promise_in_bounds"))
        b = [jnp.where(inside, z[t], z[t + 1]) for t in range(tiles + 1)]
        sums = [lon_w[0] * b[t] for t in range(tiles)]
        for k in range(1, 4):
            moved = [pltpu.roll(v, LANES - k, 1) for v in b]
            for t in range(tiles):
                sums[t] = sums[t] + lon_w[k] * jnp.where(lane < LANES - k, moved[t], moved[t + 1])
        for t in range(tiles):
            ext[f, SUB:SUB + rows, t * LANES:(t + 1) * LANES] = sums[t]
        up, down = lat_copies(f)
        if f == 0:
            pl.when(has_hi)(lambda: pl.semaphore_wait(ready.at[2], 1))
        pl.when(has_hi)(up.start)
        pl.when(has_lo)(down.start)

    for f in range(fields):
        low = jnp.zeros((SUB, width), jnp.float32)
        high = jnp.zeros((SUB, width), jnp.float32)
        for s in range(rows):
            line = ext[f, SUB + s:SUB + s + 1, :]
            if s < SUB + ABOVE:
                low = low + coef[s][:SUB] * line
            if s >= SUB - BELOW:
                high = high + coef[s][SUB:] * line
        partial.append((low, high))

    for f in range(fields):
        low, high = partial[f]
        up, down = lat_copies(f)
        pl.when(has_lo)(up.wait_recv)
        pl.when(has_hi)(down.wait_recv)
        for s in range(-BELOW, 0):
            low = low + coef[s][:SUB] * ext[f, SUB + s:SUB + s + 1, :]
        for s in range(rows, rows + ABOVE):
            high = high + coef[s][SUB:] * ext[f, SUB + s:SUB + s + 1, :]
        out[f, 0:SUB, :] = low
        out[f, SUB:rows, :] = high

    for f in range(fields):
        for copy in lon_copies[f]:
            copy.wait_send()
        up, down = lat_copies(f)
        pl.when(has_hi)(up.wait_send)
        pl.when(has_lo)(down.wait_send)


def per_device(n_lat, n_lon, tracers, lon_offsets, lon_weights, lat_offsets, lat_weights):
    rows, width = tracers.shape[2:]
    fields = tracers.shape[0] * tracers.shape[1]
    nlat = lat_offsets.shape[0]
    vmem = pl.BlockSpec(memory_space=pltpu.VMEM)
    out = pl.pallas_call(
        functools.partial(kernel, n_lat, n_lon, nlat),
        out_shape=pltpu.VMEM((fields, rows, width), jnp.float32),
        in_specs=[pl.BlockSpec(memory_space=pl.ANY)] * 5,
        out_specs=vmem,
        scratch_shapes=[
            pltpu.VMEM((fields, rows, width), jnp.float32),
            pltpu.VMEM((1, rows), jnp.int32),
            pltpu.VMEM((4, rows), jnp.float32),
            pltpu.VMEM((1, nlat), jnp.int32),
            pltpu.VMEM((4, nlat), jnp.float32),
            pltpu.VMEM((fields, rows + SUB, LANES), jnp.float32),
            pltpu.VMEM((fields, rows + SUB, LANES), jnp.float32),
            pltpu.VMEM((fields, rows + SUB, LANES), jnp.float32),
            pltpu.VMEM((fields, rows + SUB, LANES), jnp.float32),
            pltpu.VMEM((fields, rows + 2 * SUB, width), jnp.float32),
            pltpu.SemaphoreType.DMA,
            pltpu.SemaphoreType.DMA((4,)),
            pltpu.SemaphoreType.DMA((2, fields)),
            pltpu.SemaphoreType.DMA((2, fields)),
            pltpu.SemaphoreType.DMA((2, fields)),
            pltpu.SemaphoreType.DMA((2, fields)),
            pltpu.SemaphoreType.REGULAR((3,)),
        ],
        compiler_params=pltpu.CompilerParams(collective_id=0, has_side_effects=True),
    )(
        tracers.reshape(fields, rows, width),
        lon_offsets.reshape(1, rows),
        lon_weights,
        lat_offsets.reshape(1, nlat),
        lat_weights,
    )
    return out.reshape(tracers.shape)


def solution(mesh):
    return jax.shard_map(
        functools.partial(per_device, mesh.shape["lat"], mesh.shape["lon"]),
        mesh=mesh,
        in_specs=(P(None, None, "lat", "lon"), P("lat"), P(None, "lat"), P(), P()),
        out_specs=P(None, None, "lat", "lon"),
        check_vma=False,
    )
```

```python
import functools

import jax
import jax.numpy as jnp
from jax import lax
from jax.experimental import pallas as pl
from jax.experimental.pallas import tpu as pltpu
from jax.sharding import PartitionSpec as P

MESH = pl.DeviceIdType.MESH
LANES = 128
HALF = 64
SUB = 8
BELOW = 5
ABOVE = 6


def kernel(n_lat, n_lon, nlat, tr, lono_in, lonw_in, lato_in, latw_in, out,
           own, lono, lonw, lato, latw, send_r, send_l, from_l, from_r, ext,
           own_sem, s_par, s_lon, r_lon, s_lat, r_lat, ready):
    fields, rows, width = own.shape
    tiles = width // LANES
    ilat = lax.axis_index("lat")
    ilon = lax.axis_index("lon")
    right = lax.rem(ilon + 1, n_lon)
    left = lax.rem(ilon + n_lon - 1, n_lon)
    has_lo = ilat > 0
    has_hi = ilat < n_lat - 1

    barrier = pltpu.get_barrier_semaphore()
    at_first = ilon == 0
    at_last = ilon == n_lon - 1

    def signal(semaphore, lat, lon):
        pl.semaphore_signal(semaphore, inc=1, device_id=(lat, lon), device_id_type=MESH)

    pl.when(at_first)(lambda: signal(barrier, ilat, left))
    pl.when(jnp.logical_not(at_last))(lambda: signal(barrier, ilat, right))
    pl.when(has_hi)(lambda: signal(barrier, ilat + 1, ilon))

    blocks = [pltpu.make_async_copy(tr.at[f], own.at[f], own_sem.at[f]) for f in range(fields)]
    for copy in blocks:
        copy.start()
    loads = [
        pltpu.make_async_copy(source, target, s_par.at[i])
        for i, (source, target) in enumerate(
            ((lono_in, lono), (lonw_in, lonw), (lato_in, lato), (latw_in, latw)))
    ]
    for copy in loads:
        copy.start()

    greeted = has_lo.astype(jnp.int32) + jnp.logical_not(at_first).astype(jnp.int32) + at_last.astype(jnp.int32)
    pl.when(greeted > 0)(lambda: pl.semaphore_wait(barrier, greeted))
    pl.when(at_last)(lambda: signal(ready.at[0], ilat, right))
    pl.when(jnp.logical_not(at_first))(lambda: signal(ready.at[1], ilat, left))
    pl.when(has_lo)(lambda: signal(ready.at[2], ilat - 1, ilon))

    @pl.when(jnp.logical_not(has_lo))
    def _():
        ext[:, 0:SUB, :] = jnp.zeros((fields, SUB, width), jnp.float32)

    @pl.when(jnp.logical_not(has_hi))
    def _():
        ext[:, SUB + rows:, :] = jnp.zeros((fields, SUB, width), jnp.float32)

    lane8 = lax.broadcasted_iota(jnp.int32, (SUB, LANES), 1)
    upper8 = lane8 >= HALF
    last = width - LANES

    def start_right(f):
        lon_copies[f][0].start()

    def start_left(f):
        lon_copies[f][1].start()

    lon_copies = []
    for f in range(fields):
        lon_copies.append((
            pltpu.make_async_remote_copy(
                src_ref=send_r.at[f], dst_ref=from_l.at[f], send_sem=s_lon.at[0, f],
                recv_sem=r_lon.at[0, f], device_id=(ilat, right), device_id_type=MESH),
            pltpu.make_async_remote_copy(
                src_ref=send_l.at[f], dst_ref=from_r.at[f], send_sem=s_lon.at[1, f],
                recv_sem=r_lon.at[1, f], device_id=(ilat, left), device_id_type=MESH)))

    for f in range(fields):
        blocks[f].wait()
        send_r[f, 0:rows, :] = own[f, :, last:]
        a = own[f, 0:SUB, last - LANES:last]
        b = own[f, SUB:rows, last - LANES:last]
        send_r[f, rows:, :] = jnp.where(upper8, a, pltpu.roll(b, HALF, 1))
        pl.when(at_last)(functools.partial(start_right, f))
        send_l[f, 0:rows, :] = own[f, :, 0:LANES]
        a = own[f, 0:SUB, LANES:2 * LANES]
        b = own[f, SUB:rows, LANES:2 * LANES]
        send_l[f, rows:, :] = jnp.where(upper8, pltpu.roll(b, HALF, 1), a)
        pl.when(jnp.logical_not(at_first | at_last))(functools.partial(start_left, f))

    @pl.when(at_last)
    def _():
        for f in range(fields):
            start_left(f)

    @pl.when(jnp.logical_not(at_last))
    def _():
        pl.semaphore_wait(ready.at[1], 1)
        for f in range(fields):
            start_right(f)

    @pl.when(at_first)
    def _():
        pl.semaphore_wait(ready.at[0], 1)
        for f in range(fields):
            start_left(f)

    for copy in loads:
        copy.wait()

    row = lax.broadcasted_iota(jnp.int32, (rows, 1), 0)
    start = ilat * rows

    def column(values, first):
        lanes = values.shape[1]
        pick = (lax.broadcasted_iota(jnp.int32, (rows, lanes), 1)
                == first + lax.broadcasted_iota(jnp.int32, (rows, lanes), 0))
        return jnp.sum(jnp.where(pick, values, 0.0), axis=1, keepdims=True)

    lon_off = column(lono[...].astype(jnp.float32), 0).astype(jnp.int32)
    lon_w = [column(lonw[k:k + 1, :], 0) for k in range(4)]
    lat_off = column(lato[...].astype(jnp.float32), start).astype(jnp.int32)
    lat_w = [column(latw[k:k + 1, :], start) for k in range(4)]

    source = [jnp.clip(start + row - lat_off - 1 + k, 0, nlat - 1) - start for k in range(4)]

    def coefficient(s):
        total = jnp.zeros((rows, 1), jnp.float32)
        for k in range(4):
            total = total + jnp.where(source[k] == s, lat_w[k], 0.0)
        return total

    coef = {s: coefficient(s) for s in range(-BELOW, rows + ABOVE)}

    first = jnp.broadcast_to(2 * LANES - 1 - lon_off, (rows, LANES))
    coarse = first >> 7
    fine = first & (LANES - 1)
    lane = lax.broadcasted_iota(jnp.int32, (rows, LANES), 1)
    index = (lane + fine) & (LANES - 1)
    inside = lane < LANES - fine
    is_q = [coarse == q for q in range(3)]

    def lat_copies(f):
        up = pltpu.make_async_remote_copy(
            src_ref=ext.at[f, pl.ds(rows, SUB)], dst_ref=ext.at[f, pl.ds(0, SUB)],
            send_sem=s_lat.at[0, f], recv_sem=r_lat.at[0, f],
            device_id=(ilat + 1, ilon), device_id_type=MESH)
        down = pltpu.make_async_remote_copy(
            src_ref=ext.at[f, pl.ds(SUB, SUB)], dst_ref=ext.at[f, pl.ds(SUB + rows, SUB)],
            send_sem=s_lat.at[1, f], recv_sem=r_lat.at[1, f],
            device_id=(ilat - 1, ilon), device_id_type=MESH)
        return up, down

    partial = []
    for f in range(fields):
        to_r, to_l = lon_copies[f]
        to_r.wait_recv()
        to_l.wait_recv()
        tail_l = from_l[f, rows:, :]
        tail_r = from_r[f, rows:, :]
        x = [jnp.concatenate([tail_l, pltpu.roll(tail_l, HALF, 1)], axis=0), from_l[f, 0:rows, :]]
        x += [own[f, :, i * LANES:(i + 1) * LANES] for i in range(tiles)]
        x += [from_r[f, 0:rows, :], jnp.concatenate([tail_r, pltpu.roll(tail_r, HALF, 1)], axis=0)]
        z = []
        for t in range(tiles + 2):
            y = x[min(t + 3, tiles + 3)]
            for q in (2, 1, 0):
                y = jnp.where(is_q[q], x[t + q], y)
            z.append(jnp.take_along_axis(y, index, axis=1, mode="promise_in_bounds"))
        b = [jnp.where(inside, z[t], z[t + 1]) for t in range(tiles + 1)]
        sums = [lon_w[0] * b[t] for t in range(tiles)]
        for k in range(1, 4):
            moved = [pltpu.roll(v, LANES - k, 1) for v in b]
            for t in range(tiles):
                sums[t] = sums[t] + lon_w[k] * jnp.where(lane < LANES - k, moved[t], moved[t + 1])
        for t in range(tiles):
            ext[f, SUB:SUB + rows, t * LANES:(t + 1) * LANES] = sums[t]
        up, down = lat_copies(f)
        if f == 0:
            pl.when(has_hi)(lambda: pl.semaphore_wait(ready.at[2], 1))
        pl.when(has_hi)(up.start)
        pl.when(has_lo)(down.start)

    for f in range(fields):
        low = jnp.zeros((SUB, width), jnp.float32)
        high = jnp.zeros((SUB, width), jnp.float32)
        for s in range(rows):
            line = ext[f, SUB + s:SUB + s + 1, :]
            if s < SUB + ABOVE:
                low = low + coef[s][:SUB] * line
            if s >= SUB - BELOW:
                high = high + coef[s][SUB:] * line
        partial.append((low, high))

    for f in range(fields):
        low, high = partial[f]
        up, down = lat_copies(f)
        pl.when(has_lo)(up.wait_recv)
        pl.when(has_hi)(down.wait_recv)
        for s in range(-BELOW, 0):
            low = low + coef[s][:SUB] * ext[f, SUB + s:SUB + s + 1, :]
        for s in range(rows, rows + ABOVE):
            high = high + coef[s][SUB:] * ext[f, SUB + s:SUB + s + 1, :]
        out[f, 0:SUB, :] = low
        out[f, SUB:rows, :] = high

    for f in range(fields):
        for copy in lon_copies[f]:
            copy.wait_send()
        up, down = lat_copies(f)
        pl.when(has_hi)(up.wait_send)
        pl.when(has_lo)(down.wait_send)


def per_device(n_lat, n_lon, tracers, lon_offsets, lon_weights, lat_offsets, lat_weights):
    rows, width = tracers.shape[2:]
    fields = tracers.shape[0] * tracers.shape[1]
    nlat = lat_offsets.shape[0]
    vmem = pl.BlockSpec(memory_space=pltpu.VMEM)
    out = pl.pallas_call(
        functools.partial(kernel, n_lat, n_lon, nlat),
        out_shape=pltpu.VMEM((fields, rows, width), jnp.float32),
        in_specs=[pl.BlockSpec(memory_space=pl.ANY)] * 5,
        out_specs=vmem,
        scratch_shapes=[
            pltpu.VMEM((fields, rows, width), jnp.float32),
            pltpu.VMEM((1, rows), jnp.int32),
            pltpu.VMEM((4, rows), jnp.float32),
            pltpu.VMEM((1, nlat), jnp.int32),
            pltpu.VMEM((4, nlat), jnp.float32),
            pltpu.VMEM((fields, rows + SUB, LANES), jnp.float32),
            pltpu.VMEM((fields, rows + SUB, LANES), jnp.float32),
            pltpu.VMEM((fields, rows + SUB, LANES), jnp.float32),
            pltpu.VMEM((fields, rows + SUB, LANES), jnp.float32),
            pltpu.VMEM((fields, rows + 2 * SUB, width), jnp.float32),
            pltpu.SemaphoreType.DMA((fields,)),
            pltpu.SemaphoreType.DMA((4,)),
            pltpu.SemaphoreType.DMA((2, fields)),
            pltpu.SemaphoreType.DMA((2, fields)),
            pltpu.SemaphoreType.DMA((2, fields)),
            pltpu.SemaphoreType.DMA((2, fields)),
            pltpu.SemaphoreType.REGULAR((3,)),
        ],
        compiler_params=pltpu.CompilerParams(collective_id=0, has_side_effects=True),
    )(
        tracers.reshape(fields, rows, width),
        lon_offsets.reshape(1, rows),
        lon_weights,
        lat_offsets.reshape(1, nlat),
        lat_weights,
    )
    return out.reshape(tracers.shape)


def solution(mesh):
    return jax.shard_map(
        functools.partial(per_device, mesh.shape["lat"], mesh.shape["lon"]),
        mesh=mesh,
        in_specs=(P(None, None, "lat", "lon"), P("lat"), P(None, "lat"), P(), P()),
        out_specs=P(None, None, "lat", "lon"),
        check_vma=False,
    )
```

```python
import functools

import jax
import jax.numpy as jnp
from jax import lax
from jax.experimental import pallas as pl
from jax.experimental.pallas import tpu as pltpu
from jax.sharding import PartitionSpec as P

MESH = pl.DeviceIdType.MESH
LANES = 128
HALF = 64
SUB = 8
BELOW = 5
ABOVE = 6


def kernel(n_lat, n_lon, nlat, tr, lono_in, lonw_in, lato_in, latw_in, out,
           own, lono, lonw, lato, latw, send_r, send_l, from_l, from_r, ext,
           own_sem, s_par, s_lon, r_lon, s_lat, r_lat, ready):
    fields, rows, width = own.shape
    tiles = width // LANES
    ilat = lax.axis_index("lat")
    ilon = lax.axis_index("lon")
    right = lax.rem(ilon + 1, n_lon)
    left = lax.rem(ilon + n_lon - 1, n_lon)
    has_lo = ilat > 0
    has_hi = ilat < n_lat - 1

    blocks = [pltpu.make_async_copy(tr.at[f], own.at[f], own_sem.at[f]) for f in range(fields)]
    for copy in blocks:
        copy.start()

    barrier = pltpu.get_barrier_semaphore()
    at_first = ilon == 0
    at_last = ilon == n_lon - 1

    def signal(semaphore, lat, lon):
        pl.semaphore_signal(semaphore, inc=1, device_id=(lat, lon), device_id_type=MESH)

    pl.when(at_first)(lambda: signal(barrier, ilat, left))
    pl.when(jnp.logical_not(at_last))(lambda: signal(barrier, ilat, right))
    pl.when(has_hi)(lambda: signal(barrier, ilat + 1, ilon))

    loads = [
        pltpu.make_async_copy(source, target, s_par.at[i])
        for i, (source, target) in enumerate(
            ((lono_in, lono), (lonw_in, lonw), (lato_in, lato), (latw_in, latw)))
    ]
    for copy in loads:
        copy.start()

    greeted = has_lo.astype(jnp.int32) + jnp.logical_not(at_first).astype(jnp.int32) + at_last.astype(jnp.int32)
    pl.when(greeted > 0)(lambda: pl.semaphore_wait(barrier, greeted))
    pl.when(at_last)(lambda: signal(ready.at[0], ilat, right))
    pl.when(jnp.logical_not(at_first))(lambda: signal(ready.at[1], ilat, left))
    pl.when(has_lo)(lambda: signal(ready.at[2], ilat - 1, ilon))

    @pl.when(jnp.logical_not(has_lo))
    def _():
        ext[:, 0:SUB, :] = jnp.zeros((fields, SUB, width), jnp.float32)

    @pl.when(jnp.logical_not(has_hi))
    def _():
        ext[:, SUB + rows:, :] = jnp.zeros((fields, SUB, width), jnp.float32)

    lane8 = lax.broadcasted_iota(jnp.int32, (SUB, LANES), 1)
    upper8 = lane8 >= HALF
    last = width - LANES

    def start_right(f):
        lon_copies[f][0].start()

    def start_left(f):
        lon_copies[f][1].start()

    lon_copies = []
    for f in range(fields):
        lon_copies.append((
            pltpu.make_async_remote_copy(
                src_ref=send_r.at[f], dst_ref=from_l.at[f], send_sem=s_lon.at[0, f],
                recv_sem=r_lon.at[0, f], device_id=(ilat, right), device_id_type=MESH),
            pltpu.make_async_remote_copy(
                src_ref=send_l.at[f], dst_ref=from_r.at[f], send_sem=s_lon.at[1, f],
                recv_sem=r_lon.at[1, f], device_id=(ilat, left), device_id_type=MESH)))

    for f in range(fields):
        blocks[f].wait()
        send_r[f, 0:rows, :] = own[f, :, last:]
        a = own[f, 0:SUB, last - LANES:last]
        b = own[f, SUB:rows, last - LANES:last]
        send_r[f, rows:, :] = jnp.where(upper8, a, pltpu.roll(b, HALF, 1))
        pl.when(at_last)(functools.partial(start_right, f))
        send_l[f, 0:rows, :] = own[f, :, 0:LANES]
        a = own[f, 0:SUB, LANES:2 * LANES]
        b = own[f, SUB:rows, LANES:2 * LANES]
        send_l[f, rows:, :] = jnp.where(upper8, pltpu.roll(b, HALF, 1), a)
        pl.when(jnp.logical_not(at_first | at_last))(functools.partial(start_left, f))

    @pl.when(at_last)
    def _():
        for f in range(fields):
            start_left(f)

    @pl.when(jnp.logical_not(at_last))
    def _():
        pl.semaphore_wait(ready.at[1], 1)
        for f in range(fields):
            start_right(f)

    @pl.when(at_first)
    def _():
        pl.semaphore_wait(ready.at[0], 1)
        for f in range(fields):
            start_left(f)

    for copy in loads:
        copy.wait()

    row = lax.broadcasted_iota(jnp.int32, (rows, 1), 0)
    start = ilat * rows

    def column(values, first):
        lanes = values.shape[1]
        pick = (lax.broadcasted_iota(jnp.int32, (rows, lanes), 1)
                == first + lax.broadcasted_iota(jnp.int32, (rows, lanes), 0))
        return jnp.sum(jnp.where(pick, values, 0.0), axis=1, keepdims=True)

    lon_off = column(lono[...].astype(jnp.float32), 0).astype(jnp.int32)
    lon_w = [column(lonw[k:k + 1, :], 0) for k in range(4)]
    lat_off = column(lato[...].astype(jnp.float32), start).astype(jnp.int32)
    lat_w = [column(latw[k:k + 1, :], start) for k in range(4)]

    source = [jnp.clip(start + row - lat_off - 1 + k, 0, nlat - 1) - start for k in range(4)]

    def coefficient(s):
        total = jnp.zeros((rows, 1), jnp.float32)
        for k in range(4):
            total = total + jnp.where(source[k] == s, lat_w[k], 0.0)
        return total

    coef = {s: coefficient(s) for s in range(-BELOW, rows + ABOVE)}

    first = jnp.broadcast_to(2 * LANES - 1 - lon_off, (rows, LANES))
    coarse = first >> 7
    fine = first & (LANES - 1)
    lane = lax.broadcasted_iota(jnp.int32, (rows, LANES), 1)
    index = (lane + fine) & (LANES - 1)
    inside = lane < LANES - fine
    is_q = [coarse == q for q in range(3)]

    def lat_copies(f):
        up = pltpu.make_async_remote_copy(
            src_ref=ext.at[f, pl.ds(rows, SUB)], dst_ref=ext.at[f, pl.ds(0, SUB)],
            send_sem=s_lat.at[0, f], recv_sem=r_lat.at[0, f],
            device_id=(ilat + 1, ilon), device_id_type=MESH)
        down = pltpu.make_async_remote_copy(
            src_ref=ext.at[f, pl.ds(SUB, SUB)], dst_ref=ext.at[f, pl.ds(SUB + rows, SUB)],
            send_sem=s_lat.at[1, f], recv_sem=r_lat.at[1, f],
            device_id=(ilat - 1, ilon), device_id_type=MESH)
        return up, down

    partial = []
    for f in range(fields):
        to_r, to_l = lon_copies[f]
        to_l.wait_recv()
        to_r.wait_recv()
        tail_l = from_l[f, rows:, :]
        tail_r = from_r[f, rows:, :]
        x = [jnp.concatenate([tail_l, pltpu.roll(tail_l, HALF, 1)], axis=0), from_l[f, 0:rows, :]]
        x += [own[f, :, i * LANES:(i + 1) * LANES] for i in range(tiles)]
        x += [from_r[f, 0:rows, :], jnp.concatenate([tail_r, pltpu.roll(tail_r, HALF, 1)], axis=0)]
        z = []
        for t in range(tiles + 2):
            y = x[min(t + 3, tiles + 3)]
            for q in (2, 1, 0):
                y = jnp.where(is_q[q], x[t + q], y)
            z.append(jnp.take_along_axis(y, index, axis=1, mode="promise_in_bounds"))
        b = [jnp.where(inside, z[t], z[t + 1]) for t in range(tiles + 1)]
        sums = [lon_w[0] * b[t] for t in range(tiles)]
        for k in range(1, 4):
            moved = [pltpu.roll(v, LANES - k, 1) for v in b]
            for t in range(tiles):
                sums[t] = sums[t] + lon_w[k] * jnp.where(lane < LANES - k, moved[t], moved[t + 1])
        for t in range(tiles):
            ext[f, SUB:SUB + rows, t * LANES:(t + 1) * LANES] = sums[t]
        up, down = lat_copies(f)
        pl.when(has_lo)(down.start)
        if f == 0:
            pl.when(has_hi)(lambda: pl.semaphore_wait(ready.at[2], 1))
        pl.when(has_hi)(up.start)

    for f in range(fields):
        low = jnp.zeros((SUB, width), jnp.float32)
        high = jnp.zeros((SUB, width), jnp.float32)
        for s in range(rows):
            line = ext[f, SUB + s:SUB + s + 1, :]
            if s < SUB + ABOVE:
                low = low + coef[s][:SUB] * line
            if s >= SUB - BELOW:
                high = high + coef[s][SUB:] * line
        partial.append((low, high))

    for f in range(fields):
        low, high = partial[f]
        up, down = lat_copies(f)
        pl.when(has_lo)(up.wait_recv)
        pl.when(has_hi)(down.wait_recv)
        for s in range(-BELOW, 0):
            low = low + coef[s][:SUB] * ext[f, SUB + s:SUB + s + 1, :]
        for s in range(rows, rows + ABOVE):
            high = high + coef[s][SUB:] * ext[f, SUB + s:SUB + s + 1, :]
        out[f, 0:SUB, :] = low
        out[f, SUB:rows, :] = high

    for f in range(fields):
        for copy in lon_copies[f]:
            copy.wait_send()
        up, down = lat_copies(f)
        pl.when(has_hi)(up.wait_send)
        pl.when(has_lo)(down.wait_send)


def per_device(n_lat, n_lon, tracers, lon_offsets, lon_weights, lat_offsets, lat_weights):
    rows, width = tracers.shape[2:]
    fields = tracers.shape[0] * tracers.shape[1]
    nlat = lat_offsets.shape[0]
    vmem = pl.BlockSpec(memory_space=pltpu.VMEM)
    out = pl.pallas_call(
        functools.partial(kernel, n_lat, n_lon, nlat),
        out_shape=pltpu.VMEM((fields, rows, width), jnp.float32),
        in_specs=[pl.BlockSpec(memory_space=pl.ANY)] * 5,
        out_specs=vmem,
        scratch_shapes=[
            pltpu.VMEM((fields, rows, width), jnp.float32),
            pltpu.VMEM((1, rows), jnp.int32),
            pltpu.VMEM((4, rows), jnp.float32),
            pltpu.VMEM((1, nlat), jnp.int32),
            pltpu.VMEM((4, nlat), jnp.float32),
            pltpu.VMEM((fields, rows + SUB, LANES), jnp.float32),
            pltpu.VMEM((fields, rows + SUB, LANES), jnp.float32),
            pltpu.VMEM((fields, rows + SUB, LANES), jnp.float32),
            pltpu.VMEM((fields, rows + SUB, LANES), jnp.float32),
            pltpu.VMEM((fields, rows + 2 * SUB, width), jnp.float32),
            pltpu.SemaphoreType.DMA((fields,)),
            pltpu.SemaphoreType.DMA((4,)),
            pltpu.SemaphoreType.DMA((2, fields)),
            pltpu.SemaphoreType.DMA((2, fields)),
            pltpu.SemaphoreType.DMA((2, fields)),
            pltpu.SemaphoreType.DMA((2, fields)),
            pltpu.SemaphoreType.REGULAR((3,)),
        ],
        compiler_params=pltpu.CompilerParams(collective_id=0, has_side_effects=True),
    )(
        tracers.reshape(fields, rows, width),
        lon_offsets.reshape(1, rows),
        lon_weights,
        lat_offsets.reshape(1, nlat),
        lat_weights,
    )
    return out.reshape(tracers.shape)


def solution(mesh):
    return jax.shard_map(
        functools.partial(per_device, mesh.shape["lat"], mesh.shape["lon"]),
        mesh=mesh,
        in_specs=(P(None, None, "lat", "lon"), P("lat"), P(None, "lat"), P(), P()),
        out_specs=P(None, None, "lat", "lon"),
        check_vma=False,
    )
```
